512 devices in a mesh: grp: 8 (over x, core), seq: 16 (over z), voc: 4 (over y).
Axes of the slice: x: 4, y: 4, z: 16, core: 2. Of those that a mesh axis runs over, the one named last changes fastest.
Arguments:
- prompt_kv: bfloat16 [8, 2048, 1024], P('grp', 'seq', 'voc'), may hold values from -6 to 6
- owner: int32 [8, 16], P('grp'), may hold values from 0 to 7, as said below
- queries: bfloat16 [8, 16, 64, 4096], P('grp', 'seq', None, 'voc'), may hold values from -120 to 120
- resp_kv: bfloat16 [8, 16, 64, 1024], P('grp', 'seq', None, 'voc'), may hold values from -6 to 6
- lengths: int32 [8, 16], P('grp', 'seq'), may hold values from 1 to 64, as said below
- out_proj: bfloat16 [4096, 5120], P('voc', 'seq'), may hold values from -0.09375 to 0.09375
- resid: bfloat16 [8, 16, 64, 5120], P('grp', 'seq'), may hold values from -6 to 6
- gain: bfloat16 [5120], replicated, may hold values from 0.5 to 1.5
- head_w: bfloat16 [1024, 5120], P('voc'), may hold values from -4 to 4
- token_ids: int32 [8, 16, 64], P('grp', 'seq'), may hold values from 0 to 1023
- pol_logprobs: float32 [8, 16, 64], P('grp', 'seq'), may hold values from -9 to -5
Outputs:
- ref_logprobs: float32 [8, 16, 64], P('grp', 'seq')
- token_kl: float32 [8, 16, 64], P('grp', 'seq')
The draws below stay inside these ranges and needn't reach their ends.
Inputs may be any that keep to these rules, and one draw needn't show every extreme that they name: `owner`: every prompt index names exactly 16 responses. `lengths`: some response has exactly 64 valid tokens.
All inputs are finite; a program needn't handle non-finite values.
Results may differ from the reference program's by a relative error of at most 0.004.
Values may be sent and summed in bfloat16 or wider, within the bound.
A program may use at most 64 MiB of HBM per device.

```python
import math
import jax
import jax.numpy as jnp
from jax import lax

D = 5120
HD = 128
KVH = 4
QPK = 8
PT = 128
RT = 64
P_SIZE = 2048
V = 1024
PROMPTS = 8
GROUP = 16
N_GRP = 8
N_SEQ = 16


def shared_keys(key):
    return jnp.clip(jax.random.normal(key, (N_GRP, N_SEQ, RT, KVH, 1, HD), jnp.float32), -6.0, 6.0)


def draw_owner(key, part):
    key = jax.random.fold_in(key, 3)
    order = jax.random.permutation(key, N_GRP * N_SEQ)
    return (order // N_SEQ).reshape(N_GRP, N_SEQ).astype(jnp.int32)


def draw_lengths(key, part):
    key = jax.random.fold_in(key, 5)
    counts = jax.random.randint(key, (N_GRP, N_SEQ), 1, RT + 1)
    return counts.at[0, 0].set(RT).astype(jnp.int32)


def draw_resp_kv(key, part):
    base_keys = shared_keys(key)
    key = jax.random.fold_in(key, 7)
    values = jnp.clip(jax.random.normal(key, base_keys.shape, jnp.float32), -6.0, 6.0)
    return jnp.concatenate([base_keys, values], axis=4).reshape(N_GRP, N_SEQ, RT, KVH * 2 * HD).astype(jnp.bfloat16)


def draw_queries(key, part):
    key = jax.random.fold_in(key, 11)
    dims = (N_GRP, N_SEQ, RT, KVH, QPK, HD)
    mixed = 2.5 * jnp.clip(jax.random.normal(key, dims, jnp.float32), -6.0, 6.0)
    return mixed.reshape(N_GRP, N_SEQ, RT, KVH * QPK * HD).astype(jnp.bfloat16)


def draw_resid(key, part):
    key = jax.random.fold_in(key, 17)
    noise = 0.25 * jnp.clip(jax.random.normal(key, (N_GRP, N_SEQ, RT, D), jnp.float32), -6.0, 6.0)
    lift = jnp.where(jnp.arange(RT) % 8 == 5, 4.0, 0.0).reshape(1, 1, RT, 1)
    return (noise + lift).astype(jnp.bfloat16)


def draw_head_w(key, part):
    key = jax.random.fold_in(key, 13)
    noise = jnp.clip(jax.random.normal(key, (V, D), jnp.float32), -6.0, 6.0) * (3.0 / math.sqrt(D))
    offset = (90.0 + 40.0 * jax.random.uniform(jax.random.fold_in(key, 2), (V, 1), jnp.float32)) / D
    return jnp.clip(noise + offset, -4.0, 4.0).astype(jnp.bfloat16)


def with_ends(values, stream_key, smallest, largest):
    longest = values.shape.index(max(values.shape))
    spots = []
    for shift in (0, 1):
        where = [jax.random.randint(jax.random.fold_in(stream_key, axis), (), 0, length) for axis, length in enumerate(values.shape)]
        where[longest] = (where[longest] + shift) % values.shape[longest]
        spots.append(tuple(where))
    return values.at[spots[0]].set(smallest).at[spots[1]].set(largest)


def level_of(rng, extent, pieces, smallest, high):
    level, own = 1.0, jax.random.fold_in(rng, 6)
    for dim, shards_of in pieces:
        heights = jnp.exp(jax.random.uniform(jax.random.fold_in(own, dim), (shards_of,), jnp.float32, smallest / len(pieces), high / len(pieces)))
        level = level * jnp.repeat(heights, extent[dim] // shards_of).reshape([-1 if axis == dim else 1 for axis in range(len(extent))])
    return level


def centred(stream_key, shape, deviation, bound, pieces=(), held_as=jnp.bfloat16):
    values = deviation * jax.random.normal(stream_key, shape, jnp.float32)
    if pieces:
        values = values * level_of(stream_key, shape, pieces, -0.22, 0.18)
    return jnp.clip(values, -bound, bound).astype(held_as)


def setup_inputs(seed: int = 0) -> dict:
    key_list = jax.random.split(jax.random.key(seed), 12)
    prompt_kv = centred(key_list[0], (PROMPTS, P_SIZE, KVH * 2 * HD), 1.0, 6.0, ((0, 8), (1, 16), (2, 4)))
    owner = draw_owner(jax.random.fold_in(key_list[11], 71), 0)
    queries = draw_queries(jax.random.fold_in(key_list[11], 71), 0)
    resp_kv = draw_resp_kv(jax.random.fold_in(key_list[11], 71), 0)
    lengths = draw_lengths(jax.random.fold_in(key_list[11], 71), 0)
    out_proj = centred(key_list[5], (KVH * QPK * HD, D), (KVH * QPK * HD) ** -0.5, 0.09375, ((0, 4), (1, 16)))
    resid = draw_resid(jax.random.fold_in(key_list[11], 71), 0)
    gain = jnp.clip(1.0 + 0.1 * jax.random.normal(key_list[7], (D,), jnp.float32), 0.5, 1.5).astype(jnp.bfloat16)
    head_w = draw_head_w(jax.random.fold_in(key_list[11], 71), 0)
    token_ids = with_ends(jax.random.randint(key_list[9], (PROMPTS, GROUP, RT), 0, V), jax.random.fold_in(key_list[9], 1), 0, V - 1).astype(jnp.int32)
    pol_logprobs = jnp.clip(-9.0 + 4.0 * jax.random.uniform(key_list[10], (PROMPTS, GROUP, RT), jnp.float32) ** level_of(key_list[10], (PROMPTS, GROUP, RT), ((0, 8), (1, 16)), -0.2, 0.2), -9.0, -5.0)
    return dict(prompt_kv=prompt_kv, owner=owner, queries=queries, resp_kv=resp_kv, lengths=lengths, out_proj=out_proj, resid=resid, gain=gain, head_w=head_w, token_ids=token_ids, pol_logprobs=pol_logprobs)


def attend(query_rows, key_rows, value_rows, positions, prompt_len):
    scores = lax.dot_general(query_rows, key_rows, (((1,), (1,)), ((), ())), preferred_element_type=jnp.float32)
    scores = scores * (1.0 / math.sqrt(query_rows.shape[1]))
    columns = jnp.arange(key_rows.shape[0], dtype=jnp.int32)
    visible = (columns[None, :] < prompt_len) | (columns[None, :] - prompt_len <= positions[:, None])
    scores = jnp.where(visible, scores, -jnp.inf)
    highest = lax.optimization_barrier(jnp.max(scores, axis=1, keepdims=True))
    weights = jnp.exp(scores - highest)
    weights = (weights / lax.optimization_barrier(jnp.sum(weights, axis=1, keepdims=True))).astype(jnp.bfloat16)
    return jnp.dot(weights, value_rows, preferred_element_type=jnp.float32).astype(jnp.bfloat16)

def reference(prompt_kv, owner, queries, resp_kv, lengths, out_proj, resid, gain, head_w, token_ids, pol_logprobs):
    prompt_len = PT * N_SEQ

    def one_response(index):
        group = index // N_SEQ
        slot = index % N_SEQ
        prompt = prompt_kv[owner[group, slot]]
        query_all = queries[group, slot]
        own_rows = resp_kv[group, slot]
        positions = jnp.tile(jnp.arange(RT, dtype=jnp.int32), QPK)
        outputs = []
        for head in range(KVH):
            low = head * 2 * HD
            key_rows = jnp.concatenate([prompt[:, low:low + HD], own_rows[:, low:low + HD]], axis=0)
            value_rows = jnp.concatenate([prompt[:, low + HD:low + 2 * HD], own_rows[:, low + HD:low + 2 * HD]], axis=0)
            query_rows = query_all[:, head * QPK * HD:(head + 1) * QPK * HD]
            query_rows = query_rows.reshape(RT, QPK, HD).transpose(1, 0, 2).reshape(QPK * RT, HD)
            result = attend(query_rows, key_rows, value_rows, positions, prompt_len)
            outputs.append(result.reshape(QPK, RT, HD).transpose(1, 0, 2).reshape(RT, QPK * HD))
        attention = jnp.concatenate(outputs, axis=1)
        branch = jnp.dot(attention, out_proj, preferred_element_type=jnp.float32)
        hidden = resid[group, slot].astype(jnp.float32) + branch
        scale = lax.rsqrt(lax.optimization_barrier(jnp.mean(hidden * hidden, axis=1, keepdims=True)) + 1e-06)
        normed = (hidden * scale * gain.astype(jnp.float32)[None, :]).astype(jnp.bfloat16)
        logits = lax.dot_general(normed, head_w, (((1,), (1,)), ((), ())), preferred_element_type=jnp.float32)
        total_log = jax.nn.logsumexp(logits, axis=1)
        picked = jnp.take_along_axis(logits, token_ids[group, slot][:, None], axis=1)[:, 0]
        ref_logprob = picked - total_log
        live_rows = jnp.arange(RT, dtype=jnp.int32) < lengths[group, slot]
        delta = jnp.clip(ref_logprob - pol_logprobs[group, slot], -20.0, 20.0)
        divergence = jnp.clip(jnp.exp(delta) - delta - 1.0, -10.0, 10.0)
        zeros = jnp.zeros_like(ref_logprob)
        return (jnp.where(live_rows, ref_logprob, zeros), jnp.where(live_rows, divergence, zeros))
    ref_all, kl_all = lax.map(one_response, jnp.arange(N_GRP * N_SEQ, dtype=jnp.int32))
    return (ref_all.reshape(N_GRP, N_SEQ, RT), kl_all.reshape(N_GRP, N_SEQ, RT))
```

```python
import functools
import math

import jax
import jax.numpy as jnp
from jax import lax
from jax.experimental import pallas as pl
from jax.experimental.pallas import tpu as pltpu
from jax.sharding import PartitionSpec as P

MESH = pl.DeviceIdType.MESH
HD = 128
RT = 64
D = 5120
CW = 640
NCH = D // CW
BF = jnp.bfloat16
F32 = jnp.float32
LOG2E_SCALE = math.log2(math.e) / math.sqrt(HD)
CHUNKS = ((0, 1, 2), (3, 4, 5, 6), (7, 8, 9, 10), (11, 12, 13, 14, 15))
STARTS = (0, 512, 1024, 1536, 2176)
PLACE = {slot: (t, i) for t, slots in enumerate(CHUNKS) for i, slot in enumerate(slots)}


def slot_of(way, hop):
    return 0 if hop == 0 else 15 if hop == 8 else 2 * hop - 1 + way


def lanes_max(rows):
    high = jnp.abs(rows[:, 0:128])
    for i in range(128, rows.shape[1], 128):
        high = jnp.maximum(high, jnp.abs(rows[:, i : i + 128]))
    return jnp.broadcast_to(jnp.max(high, axis=1, keepdims=True), high.shape)


def encode(rows):
    exponent = jnp.ceil(jnp.log2(jnp.maximum(lanes_max(rows), 1e-30)) + 0.01)
    scale = jnp.exp2(-exponent) * 32000.0
    scaled = rows * jnp.concatenate([scale] * (CW // 128), axis=1)
    return jnp.concatenate([jnp.round(scaled), exponent], axis=1).astype(jnp.int16)


def decode(coded):
    scale = jnp.exp2(coded[:, CW:].astype(F32)) * (1.0 / 32000.0)
    return coded[:, :CW].astype(F32) * jnp.concatenate([scale] * (CW // 128), axis=1)


def kernel(
    kv_ref, owner_ref, q_ref, own_ref, len_ref, proj_ref, resid_ref, gain_ref, head_ref, tok_ref, pol_ref,
    ref_out, kl_out,
    kv0, kv1, kv2, kv3, packs, own_blocks, owner_in, owner_v, owner_s, m_s, l_s, probs, att_send, att_recv, att,
    v_in, w_slots, core_send, core_recv, tmp1, own1, send1, recv1, tmp2, own2, send2, recv2,
    resid_v, head_v, gain_v, tok_v, pol_v, len_s, hidden_c, squares, stats, load_sem,
    q_ss, q_rs, o_ss, o_rs, kv_ss, kv_rs, sib_ss, sib_rs, w_ss, w_rs, a_ss, a_rs, c_ss, c_rs,
    f_ss, f_rs, g_ss, g_rs, n_ss, n_rs, t_ss, t_rs, e_ss, e_rs,
):
    g, s, v = lax.axis_index("grp"), lax.axis_index("seq"), lax.axis_index("voc")
    x, c = lax.div(g, 2), lax.rem(g, 2)
    kvs = (kv0, kv1, kv2, kv3)
    sends = []

    def remote(src, dst, ss, rs, device):
        return pltpu.make_async_remote_copy(
            src_ref=src, dst_ref=dst, send_sem=ss, recv_sem=rs, device_id=device, device_id_type=MESH
        )

    def launch(copy):
        copy.start()
        sends.append(copy)

    def grp(d):
        return {"grp": lax.rem(g + d, 8)}

    def along_x(d):
        return {"grp": lax.rem(g + 2 * d, 8)}

    def along_y(d):
        return {"voc": lax.rem(v + d, 4)}

    def along_z(way):
        return {"seq": lax.rem(s + (1 if way == 0 else 15), 16)}

    sibling = {"grp": 2 * x + 1 - c}

    barrier = pltpu.get_barrier_semaphore()
    for device in [grp(d) for d in range(1, 8)] + [along_y(d) for d in range(1, 4)] + [along_z(0), along_z(1)]:
        pl.semaphore_signal(barrier, inc=1, device_id=device, device_id_type=MESH)

    def load(index, src, dst):
        copy = pltpu.make_async_copy(src, dst, load_sem.at[index])
        copy.start()
        return copy

    early = [
        load(0, owner_ref, owner_in),
        load(1, kv_ref.at[0, :, pl.ds(HD, HD)], v_in),
        load(2, kv_ref.at[0, :, pl.ds(0, HD)], kv0.at[c, 0, pl.ds(0, HD)]),
    ]
    early += [load(3 + j, q_ref.at[0, 0, :, pl.ds(j * HD, HD)], packs.at[x, pl.ds(j * RT, RT)]) for j in range(8)]
    early += [load(11 + j, own_ref.at[0, 0, :, pl.ds(j * HD, HD)], packs.at[x, pl.ds(512 + j * RT, RT)]) for j in range(2)]
    early.append(load(13, proj_ref.at[:, pl.ds(pl.multiple_of(g * HD, HD), HD)], w_slots.at[s]))
    late = [
        load(14, resid_ref.at[0, 0, pl.ds(pl.multiple_of(v * 16, 16), 16), :], resid_v),
        load(15, head_ref, head_v),
        load(16, gain_ref, gain_v),
        load(17, tok_ref, tok_v),
        load(18, pol_ref, pol_v),
        load(19, len_ref, len_s),
    ]
    for copy in early:
        copy.wait()
    kv0[c, 0, 128:256] = v_in[...].T
    owner_v[pl.ds(g, 1), :] = jnp.full((1, 128), owner_in[0, s], jnp.int32)

    pl.semaphore_wait(barrier, 12)

    def kv_piece(slot, sub):
        t, i = PLACE[slot]
        return kvs[t].at[c, i, pl.ds(sub * 128, 128)]

    def kv_copy(way, hop, sub):
        return remote(
            kv_piece(slot_of(way, hop - 1), sub), kv_piece(slot_of(way, hop), sub),
            kv_ss.at[way, hop - 1, sub], kv_rs.at[way, hop - 1, sub], along_z(way),
        )

    def kv_subs(way, hop):
        return (0, 1) if hop < 8 else (way,)

    def sib_copy(slot):
        t, i = PLACE[slot]
        return remote(kvs[t].at[c, i], kvs[t].at[c, i], sib_ss.at[slot], sib_rs.at[slot], sibling)

    def kv_hop(hop):
        for sub in (0, 1):
            for way in (0, 1):
                if sub in kv_subs(way, hop):
                    kv_copy(way, hop, sub).wait_recv()
                    if hop < 8 and sub in kv_subs(way, hop + 1):
                        launch(kv_copy(way, hop + 1, sub))
        for slot in sorted({slot_of(0, hop), slot_of(1, hop)}):
            launch(sib_copy(slot))

    def w_piece(way, hop, which):
        index = lax.rem(s + (16 - hop if way == 0 else hop), 16)
        if which == 8:
            return w_slots.at[index, pl.ds(way * 160, 160)]
        return w_slots.at[index]

    def w_copy(way, hop):
        return remote(
            w_piece(way, hop - 1, hop), w_piece(way, hop - 1, hop), w_ss.at[way, hop - 1], w_rs.at[way, hop - 1],
            along_z(way),
        )

    def w_arrived(way, hop):
        ref = w_piece(way, hop, hop)
        return remote(ref, ref, w_ss.at[way, hop - 1], w_rs.at[way, hop - 1], along_z(way))

    def w_hop(hop):
        for way in (0, 1):
            w_arrived(way, hop).wait_recv()
            if hop < 8:
                launch(w_copy(way, hop + 1))

    for sub in (0, 1):
        for way in (0, 1):
            launch(kv_copy(way, 1, sub))
    launch(sib_copy(0))
    for d in range(1, 8):
        row = owner_v.at[pl.ds(g, 1)]
        launch(remote(row, row, o_ss.at[d - 1], o_rs.at[d - 1], grp(d)))
    for d in (1, 3, 2):
        launch(remote(packs.at[x], packs.at[x], q_ss.at[d - 1], q_rs.at[d - 1], along_x(d)))

    kv_hop(1)
    kv_hop(2)

    for d in range(1, 8):
        row = owner_v.at[pl.ds(lax.rem(g + 8 - d, 8), 1)]
        remote(row, row, o_ss.at[d - 1], o_rs.at[d - 1], grp(d)).wait_recv()
    to_scalar = pltpu.make_async_copy(owner_v, owner_s, load_sem.at[20])
    to_scalar.start()
    for d in (1, 3, 2):
        ref = packs.at[lax.rem(x + 4 - d, 4)]
        remote(ref, ref, q_ss.at[d - 1], q_rs.at[d - 1], along_x(d)).wait_recv()
    to_scalar.wait()
    pad = jnp.zeros((64, 128), BF)
    for u in range(4):
        own_blocks[u, 0:64] = packs[u, 512:576]
        own_blocks[u, 64:128] = pad
        own_blocks[u, 128:256] = jnp.concatenate([packs[u, 576:640], pad], axis=0).T

    def attend(t, units):
        n = len(CHUNKS[t])
        for u in units:
            odd_prompt = lax.rem(owner_s[2 * u + c, 0], 2)
            keys = [kvs[t][odd_prompt, i, 0:128] for i in range(n)]
            if t == 0:
                keys.append(own_blocks[u, 0:128])
            keys = jnp.concatenate(keys, axis=0)
            scores = lax.dot_general(
                keys, packs[u, 0:512], (((1,), (1,)), ((), ())), preferred_element_type=F32
            )
            if t == 0:
                row = lax.broadcasted_iota(jnp.int32, (128, 512), 0)
                position = lax.broadcasted_iota(jnp.int32, (128, 512), 1) & 63
                mine = jnp.where(row <= position, scores[n * 128 :], -1e30)
                scores = jnp.concatenate([scores[: n * 128], mine], axis=0)
            high = jnp.max(scores, axis=0, keepdims=True) * LOG2E_SCALE
            if t > 0:
                before = m_s[u, t - 1 : t]
                high = jnp.maximum(before, high)
            weights = jnp.exp2(scores * LOG2E_SCALE - high)
            total = jnp.sum(weights, axis=0, keepdims=True)
            if t > 0:
                total = l_s[u, 0:1] * jnp.exp2(before - high) + total
            m_s[u, t : t + 1] = high
            l_s[u, 0:1] = total
            probs[u, STARTS[t] : STARTS[t + 1]] = weights

    def weigh(u):
        odd_prompt = lax.rem(owner_s[2 * u + c, 0], 2)
        last, inverse = m_s[u, 3:4], 1.0 / l_s[u, 0:1]
        out = jnp.zeros((128, 512), F32)
        for t in range(4):
            values = [kvs[t][odd_prompt, i, 128:256] for i in range(len(CHUNKS[t]))]
            if t == 0:
                values.append(own_blocks[u, 128:256])
            share = jnp.exp2(m_s[u, t : t + 1] - last) * inverse
            weights = (probs[u, STARTS[t] : STARTS[t + 1]] * share).astype(BF)
            out = out + jnp.dot(jnp.concatenate(values, axis=1), weights, preferred_element_type=F32)
        att_send[u] = out.T.astype(BF)

    def chunk_ready(t):
        for slot in CHUNKS[t]:
            sib_ref = kvs[t].at[1 - c, PLACE[slot][1]]
            remote(sib_ref, sib_ref, sib_ss.at[slot], sib_rs.at[slot], sibling).wait_recv()

    for way in (0, 1):
        launch(w_copy(way, 1))
    kv_hop(3)
    chunk_ready(0)
    attend(0, (0, 1))
    kv_hop(4)
    attend(0, (2, 3))
    w_hop(1)
    kv_hop(5)
    chunk_ready(1)
    attend(1, (0, 1))
    w_hop(2)
    kv_hop(6)
    attend(1, (2, 3))
    w_hop(3)
    kv_hop(7)
    chunk_ready(2)
    attend(2, (0, 1))
    w_hop(4)
    kv_hop(8)
    attend(2, (2, 3))
    w_hop(5)
    chunk_ready(3)
    attend(3, (0, 1))
    w_hop(6)
    attend(3, (2, 3))

    for u in range(4):
        weigh(u)
    for d in (1, 2, 3, 5, 6, 7, 4):
        j = lax.rem(g + d, 8)
        launch(remote(
            att_send.at[:, pl.ds(pl.multiple_of(j * RT, RT), RT), :], att_recv.at[x, c],
            a_ss.at[d - 1], a_rs.at[d - 1], grp(d),
        ))
    att_recv[x, c] = att_send[:, pl.ds(pl.multiple_of(g * RT, RT), RT), :]
    w_hop(7)
    w_hop(8)
    for d in (1, 2, 3, 5, 6, 7, 4):
        j = lax.rem(g + 8 - d, 8)
        ref = att_recv.at[lax.div(j, 2), lax.rem(j, 2)]
        remote(ref, ref, a_ss.at[d - 1], a_rs.at[d - 1], grp(d)).wait_recv()
    for cc in range(2):
        for xx in range(4):
            att[cc, xx * RT : (xx + 1) * RT] = att_recv[lax.div(owner_s[2 * xx + cc, 0], 2), cc, xx]

    def core_copy(k):
        return remote(core_send.at[k], core_recv.at[k], c_ss.at[k], c_rs.at[k], sibling)

    def first(k, d):
        me, device = (x, along_x(d)) if k % 2 == 0 else (v, along_y(d))
        return remote(
            send1.at[k, lax.rem(me + d, 4)], recv1.at[k, d - 1], f_ss.at[k, d - 1], f_rs.at[k, d - 1], device
        )

    def second(k, d):
        me, device = (v, along_y(d)) if k % 2 == 0 else (x, along_x(d))
        return remote(
            send2.at[k, lax.rem(me + d, 4)], recv2.at[k, d - 1], g_ss.at[k, d - 1], g_rs.at[k, d - 1], device
        )

    def normed_copy(k, d, from_me=True):
        ref = hidden_c.at[k, v if from_me else lax.rem(v + 4 - d, 4)]
        return remote(ref, ref, n_ss.at[k, d - 1], n_rs.at[k, d - 1], along_y(d))

    def project(rows, k):
        columns = jnp.concatenate([w_slots[2 * k], w_slots[2 * k + 1]], axis=0)
        return lax.dot_general(rows, columns, (((1,), (1,)), ((), ())), preferred_element_type=F32)

    def to_sibling(k):
        core_send[k] = encode(project(att[1 - c], k))
        launch(core_copy(k))

    def step1(k):
        core_copy(k).wait_recv()
        total = project(att[c], k) + decode(core_recv[k])
        if k % 2 == 0:
            pieces = [total[i * 64 : (i + 1) * 64] for i in range(4)]
        else:
            pieces = [
                jnp.concatenate([total[j * 64 + i * 16 : j * 64 + i * 16 + 16] for j in range(4)], axis=0)
                for i in range(4)
            ]
        for i in range(4):
            tmp1[i] = pieces[i]
            send1[k, i] = encode(pieces[i])
        for d in (1, 3, 2):
            launch(first(k, d))
        own1[k] = tmp1[x if k % 2 == 0 else v]

    def step2(k):
        total = own1[k]
        for d in (1, 3, 2):
            first(k, d).wait_recv()
        for d in (1, 3, 2):
            total = total + decode(recv1[k, d - 1])
        coded = encode(total)
        for i in range(4):
            tmp2[i] = total[i * 16 : (i + 1) * 16]
            send2[k, i] = coded[i * 16 : (i + 1) * 16]
        for d in (1, 3, 2):
            launch(second(k, d))
        own2[k] = tmp2[v if k % 2 == 0 else x]

    def step3(k, square):
        cols = slice(k * CW, (k + 1) * CW)
        total = own2[k]
        for d in (1, 3, 2):
            second(k, d).wait_recv()
        for d in (1, 3, 2):
            total = total + decode(recv2[k, d - 1])
        hidden = resid_v[:, cols].astype(F32) + total
        for i in range(CW // 128):
            part = hidden[:, i * 128 : (i + 1) * 128]
            square = square + part * part
        hidden_c[k, v] = encode(hidden)
        for d in (1, 3, 2):
            launch(normed_copy(k, d))
        return square

    def step4(k, scale, logits):
        rows = decode(jnp.concatenate([hidden_c[k, i] for i in range(4)], axis=0))
        tiles = [
            (rows[:, i * 128 : (i + 1) * 128] * scale * gain_v[k * 5 + i : k * 5 + i + 1].astype(F32)).astype(BF)
            for i in range(CW // 128)
        ]
        return logits + lax.dot_general(
            head_v[:, k * CW : (k + 1) * CW], jnp.concatenate(tiles, axis=1), (((1,), (1,)), ((), ())),
            preferred_element_type=F32,
        )

    square = jnp.zeros((16, 128), F32)
    to_sibling(0)
    to_sibling(1)
    for k in range(4):
        to_sibling(k + 2)
        step1(k)
    for copy in late:
        copy.wait()
    for p in range(0, NCH, 2):
        if p + 4 < NCH:
            if p + 6 < NCH:
                to_sibling(p + 6)
                to_sibling(p + 7)
            step1(p + 4)
            step1(p + 5)
        step2(p)
        step2(p + 1)
        if p >= 2:
            square = step3(p - 2, square)
            square = step3(p - 1, square)
    square = step3(NCH - 2, square)
    square = step3(NCH - 1, square)
    squares[v] = square
    for d in (1, 3, 2):
        launch(remote(squares.at[v], squares.at[v], t_ss.at[d - 1], t_rs.at[d - 1], along_y(d)))
    for k in range(NCH):
        for d in (1, 3, 2):
            normed_copy(k, d, False).wait_recv()
    for d in (1, 3, 2):
        ref = squares.at[lax.rem(v + 4 - d, 4)]
        remote(ref, ref, t_ss.at[d - 1], t_rs.at[d - 1], along_y(d)).wait_recv()
    rows = jnp.concatenate([squares[i] for i in range(4)], axis=0)
    mean = jnp.broadcast_to(jnp.sum(rows, axis=1, keepdims=True) * (1.0 / D), (RT, 128))
    scale = lax.rsqrt(mean + 1e-06)
    logits = jnp.zeros((256, RT), F32)
    for k in range(NCH):
        logits = step4(k, scale, logits)

    high = jnp.max(logits, axis=0, keepdims=True)
    total = jnp.sum(jnp.exp(logits - high), axis=0, keepdims=True)
    entry = lax.broadcasted_iota(jnp.int32, (256, RT), 0) + v * 256
    picked = jnp.sum(jnp.where(entry == tok_v[0], logits, 0.0), axis=0, keepdims=True)
    stats[0, 0:1, 0:RT] = high
    stats[0, 1:2, 0:RT] = total
    stats[0, 2:3, 0:RT] = picked
    for d in (1, 3, 2):
        launch(remote(stats.at[0], stats.at[d], e_ss.at[d - 1], e_rs.at[d - 1], along_y(d)))
    for d in (1, 3, 2):
        remote(stats.at[0], stats.at[d], e_ss.at[d - 1], e_rs.at[d - 1], along_y(d)).wait_recv()
    highs = [high] + [stats[d, 0:1, 0:RT] for d in (1, 2, 3)]
    totals = [total] + [stats[d, 1:2, 0:RT] for d in (1, 2, 3)]
    target = picked + stats[1, 2:3, 0:RT] + stats[2, 2:3, 0:RT] + stats[3, 2:3, 0:RT]
    highest = functools.reduce(jnp.maximum, highs)
    exp_total = functools.reduce(jnp.add, [a * jnp.exp(b - highest) for a, b in zip(totals, highs)])
    logprob = target - (highest + jnp.log(exp_total))
    live = lax.broadcasted_iota(jnp.int32, (1, RT), 1) < len_s[0, 0]
    delta = jnp.clip(logprob - pol_v[0], -20.0, 20.0)
    divergence = jnp.clip(jnp.exp(delta) - delta - 1.0, -10.0, 10.0)
    ref_out[0] = jnp.where(live, logprob, 0.0)
    kl_out[0] = jnp.where(live, divergence, 0.0)
    for copy in sends:
        copy.wait_send()


def local(prompt_kv, owner, queries, resp_kv, lengths, out_proj, resid, gain, head_w, token_ids, pol_logprobs):
    vmem, hbm = pl.BlockSpec(memory_space=pltpu.VMEM), pl.BlockSpec(memory_space=pltpu.HBM)
    dma = pltpu.SemaphoreType.DMA
    wide = CW + 128
    scratch = [
        *[pltpu.VMEM((2, len(slots), 256, 128), BF) for slots in CHUNKS],
        pltpu.VMEM((4, 640, 128), BF),
        pltpu.VMEM((4, 256, 128), BF),
        pltpu.SMEM((1, 16), jnp.int32),
        pltpu.VMEM((8, 128), jnp.int32),
        pltpu.SMEM((8, 128), jnp.int32),
        pltpu.VMEM((4, 8, 512), F32),
        pltpu.VMEM((4, 8, 512), F32),
        pltpu.VMEM((4, STARTS[4], 512), F32),
        pltpu.VMEM((4, 512, 128), BF),
        pltpu.VMEM((4, 2, 4, RT, 128), BF),
        pltpu.VMEM((2, 256, 128), BF),
        pltpu.VMEM((128, 128), BF),
        pltpu.VMEM((16, 320, 128), BF),
        pltpu.VMEM((NCH, 256, wide), jnp.int16),
        pltpu.VMEM((NCH, 256, wide), jnp.int16),
        pltpu.VMEM((4, 64, CW), F32),
        pltpu.VMEM((NCH, 64, CW), F32),
        pltpu.VMEM((NCH, 4, 64, wide), jnp.int16),
        pltpu.VMEM((NCH, 3, 64, wide), jnp.int16),
        pltpu.VMEM((4, 16, CW), F32),
        pltpu.VMEM((NCH, 16, CW), F32),
        pltpu.VMEM((NCH, 4, 16, wide), jnp.int16),
        pltpu.VMEM((NCH, 3, 16, wide), jnp.int16),
        pltpu.VMEM((16, D), BF),
        pltpu.VMEM((256, D), BF),
        pltpu.VMEM((D // 128, 128), BF),
        pltpu.VMEM((1, 1, RT), jnp.int32),
        pltpu.VMEM((1, 1, RT), F32),
        pltpu.SMEM((1, 1), jnp.int32),
        pltpu.VMEM((NCH, 4, 16, wide), jnp.int16),
        pltpu.VMEM((4, 16, 128), F32),
        pltpu.VMEM((4, 8, 128), F32),
        dma((21,)),
    ]
    for shape in ((3,), (7,), (2, 8, 2), (16,), (2, 8), (7,), (NCH,), (NCH, 3), (NCH, 3), (NCH, 3), (3,), (3,)):
        scratch += [dma(shape), dma(shape)]
    out = jax.ShapeDtypeStruct((1, 1, RT), F32)
    return pl.pallas_call(
        kernel,
        out_shape=(out, out),
        in_specs=[hbm] * 11,
        out_specs=(vmem, vmem),
        scratch_shapes=scratch,
        compiler_params=pltpu.CompilerParams(
            collective_id=0, has_side_effects=True, vmem_limit_bytes=60 * 1024 * 1024
        ),
        name="score",
    )(
        prompt_kv, owner, queries, resp_kv, lengths, out_proj.T, resid, gain.reshape(D // 128, 128), head_w, token_ids,
        pol_logprobs,
    )


def solution(mesh):
    in_specs = (
        P("grp", "seq", "voc"),
        P("grp", None),
        P("grp", "seq", None, "voc"),
        P("grp", "seq", None, "voc"),
        P("grp", "seq"),
        P("voc", "seq"),
        P("grp", "seq", None, None),
        P(),
        P("voc", None),
        P("grp", "seq", None),
        P("grp", "seq", None),
    )
    out_specs = (P("grp", "seq", None), P("grp", "seq", None))
    return jax.shard_map(local, mesh=mesh, in_specs=in_specs, out_specs=out_specs, check_vma=False)
```

```python
import functools
import math

import jax
import jax.numpy as jnp
from jax import lax
from jax.experimental import pallas as pl
from jax.experimental.pallas import tpu as pltpu
from jax.sharding import PartitionSpec as P

MESH = pl.DeviceIdType.MESH
HD = 128
RT = 64
D = 5120
CW = 640
NCH = D // CW
BF = jnp.bfloat16
F32 = jnp.float32
LOG2E_SCALE = math.log2(math.e) / math.sqrt(HD)
CHUNKS = ((0, 1, 2, 3, 4), (5, 6, 7, 8), (9, 10, 11, 12), (13, 14, 15))
STARTS = (0, 768, 1280, 1792, 2176)
X_FIRST = (False, True, False, True, True, True, True, True)
ORDER = (0, 1, 7, 2, 6, 3, 5, 4)
PLACE = {slot: (t, i) for t, slots in enumerate(CHUNKS) for i, slot in enumerate(slots)}


def slot_of(way, hop):
    return 0 if hop == 0 else 15 if hop == 8 else 2 * hop - 1 + way


def lanes_max(rows):
    high = jnp.abs(rows[:, 0:128])
    for i in range(128, rows.shape[1], 128):
        high = jnp.maximum(high, jnp.abs(rows[:, i : i + 128]))
    return jnp.broadcast_to(jnp.max(high, axis=1, keepdims=True), high.shape)


def encode(rows):
    exponent = jnp.ceil(jnp.log2(jnp.maximum(lanes_max(rows), 1e-30)) + 0.01)
    scale = jnp.exp2(-exponent) * 32000.0
    scaled = rows * jnp.concatenate([scale] * (CW // 128), axis=1)
    return jnp.concatenate([jnp.round(scaled), exponent], axis=1).astype(jnp.int16)


def decode(coded):
    scale = jnp.exp2(coded[:, CW:].astype(F32)) * (1.0 / 32000.0)
    return coded[:, :CW].astype(F32) * jnp.concatenate([scale] * (CW // 128), axis=1)


def kernel(
    kv_ref, owner_ref, q_ref, own_ref, proj_ref, resid_ref, gain_ref, head_ref, tok_ref, pol_ref,
    out_ref,
    kv0, kv1, kv2, kv3, packs, own_blocks, owner_in, owner_v, owner_s, m_s, l_s, probs, att_send, att_recv, att,
    v_in, w_slots, tmp1, own1, kept, send1, recv1, tmp2, own2, send2, recv2,
    resid_v, head_v, gain_in, gain_v, tok_v, pol_v, hidden_c, hidden_v, squares, stats, load_sem,
    q_ss, q_rs, o_ss, o_rs, kv_ss, kv_rs, sib_ss, sib_rs, w_ss, w_rs, wb_ss, wb_rs, a_ss, a_rs,
    f_ss, f_rs, g_ss, g_rs, n_ss, n_rs, t_ss, t_rs, e_ss, e_rs,
):
    g, s, v = lax.axis_index("grp"), lax.axis_index("seq"), lax.axis_index("voc")
    x, c = lax.div(g, 2), lax.rem(g, 2)
    kvs = (kv0, kv1, kv2, kv3)
    sends = []

    def remote(src, dst, ss, rs, device):
        return pltpu.make_async_remote_copy(
            src_ref=src, dst_ref=dst, send_sem=ss, recv_sem=rs, device_id=device, device_id_type=MESH
        )

    def launch(copy):
        copy.start()
        sends.append(copy)

    def along_x(d):
        return {"grp": lax.rem(g + 2 * d, 8)}

    def along_y(d):
        return {"voc": lax.rem(v + d, 4)}

    def along_z(way):
        return {"seq": lax.rem(s + (1 if way == 0 else 15), 16)}

    sibling = {"grp": 2 * x + 1 - c}

    barrier = pltpu.get_barrier_semaphore()
    for device in [along_x(d) for d in range(1, 4)] + [along_y(d) for d in range(1, 4)] + [along_z(0), along_z(1), sibling]:
        pl.semaphore_signal(barrier, inc=1, device_id=device, device_id_type=MESH)

    def load(index, src, dst):
        copy = pltpu.make_async_copy(src, dst, load_sem.at[index])
        copy.start()
        return copy

    early = [
        load(1, kv_ref.at[0, :, pl.ds(HD, HD)], v_in),
        load(2, kv_ref.at[0, :, pl.ds(0, HD)], kv0.at[c, 0, pl.ds(0, HD)]),
    ]
    early_owner = load(0, owner_ref, owner_in)
    early_q = [load(3 + j, q_ref.at[0, 0, :, pl.ds(j * HD, HD)], packs.at[x, pl.ds(j * RT, RT)]) for j in range(8)]
    early_q += [load(11 + j, own_ref.at[0, 0, :, pl.ds(j * HD, HD)], packs.at[x, pl.ds(512 + j * RT, RT)]) for j in range(2)]
    early_w = load(13, proj_ref.at[:, pl.ds(pl.multiple_of(g * HD, HD), HD)], w_slots.at[c, s])
    late = [
        load(14, resid_ref.at[0, 0, pl.ds(pl.multiple_of(v * 16, 16), 16), :], resid_v),
        load(15, head_ref, head_v),
        load(16, gain_ref, gain_in),
        load(17, tok_ref, tok_v),
        load(18, pol_ref, pol_v),
    ]
    for copy in early:
        copy.wait()
    kv0[c, 0, 128:256] = v_in[...].T

    pl.semaphore_wait(barrier, 9)

    def kv_piece(slot, sub):
        t, i = PLACE[slot]
        return kvs[t].at[c, i, pl.ds(sub * 128, 128)]

    def kv_copy(way, hop, sub):
        return remote(
            kv_piece(slot_of(way, hop - 1), sub), kv_piece(slot_of(way, hop), sub),
            kv_ss.at[way, hop - 1, sub], kv_rs.at[way, hop - 1, sub], along_z(way),
        )

    def kv_subs(way, hop):
        return (0, 1) if hop < 8 else (way,)

    def sib_copy(slot):
        t, i = PLACE[slot]
        return remote(kvs[t].at[c, i], kvs[t].at[c, i], sib_ss.at[slot], sib_rs.at[slot], sibling)

    def kv_hop(hop):
        for sub in (0, 1):
            for way in (0, 1):
                if sub in kv_subs(way, hop):
                    kv_copy(way, hop, sub).wait_recv()
                    if hop < 8 and sub in kv_subs(way, hop + 1):
                        launch(kv_copy(way, hop + 1, sub))
        for slot in sorted({slot_of(0, hop), slot_of(1, hop)}):
            launch(sib_copy(slot))

    def w_piece(way, hop, which):
        index = lax.rem(s + (16 - hop if way == 0 else hop), 16)
        if which == 8:
            return w_slots.at[c, index, pl.ds(way * 160, 160)]
        return w_slots.at[c, index]

    def w_copy(way, hop):
        return remote(
            w_piece(way, hop - 1, hop), w_piece(way, hop - 1, hop), w_ss.at[way, hop - 1], w_rs.at[way, hop - 1],
            along_z(way),
        )

    def w_arrived(way, hop):
        ref = w_piece(way, hop, hop)
        return remote(ref, ref, w_ss.at[way, hop - 1], w_rs.at[way, hop - 1], along_z(way))

    def w_hop(hop):
        for way in (0, 1):
            w_arrived(way, hop).wait_recv()
            if hop < 8:
                launch(w_copy(way, hop + 1))
        for way in (0, 1) if hop < 8 else (0,):
            launch(w_sib(way, hop, c))

    def w_sib(way, hop, head):
        ref = w_slots.at[head, lax.rem(s + (16 - hop if way == 0 else hop), 16)]
        slot = slot_of(way, hop)
        return remote(ref, ref, wb_ss.at[slot], wb_rs.at[slot], sibling)

    def w_ready(hop):
        for way in (0, 1) if 0 < hop < 8 else (0,):
            w_sib(way, hop, 1 - c).wait_recv()

    for sub in (0, 1):
        for way in (0, 1):
            launch(kv_copy(way, 1, sub))
    launch(sib_copy(0))
    for copy in early_q:
        copy.wait()
    for d in (1, 3, 2):
        launch(remote(packs.at[x], packs.at[x], q_ss.at[d - 1], q_rs.at[d - 1], along_x(d)))
    early_owner.wait()
    owner_v[pl.ds(g, 1), :] = jnp.full((1, 128), owner_in[0, s], jnp.int32)
    for d in (1, 3, 2):
        row = owner_v.at[pl.ds(g, 1)]
        launch(remote(row, row, o_ss.at[d - 1], o_rs.at[d - 1], along_x(d)))

    kv_hop(1)
    kv_hop(2)
    kv_hop(3)

    for d in (1, 3, 2):
        row = owner_v.at[pl.ds(lax.rem(g + 8 - 2 * d, 8), 1)]
        remote(row, row, o_ss.at[d - 1], o_rs.at[d - 1], along_x(d)).wait_recv()
    to_scalar = pltpu.make_async_copy(owner_v, owner_s, load_sem.at[20])
    to_scalar.start()
    for d in (1, 3, 2):
        ref = packs.at[lax.rem(x + 4 - d, 4)]
        remote(ref, ref, q_ss.at[d - 1], q_rs.at[d - 1], along_x(d)).wait_recv()
    to_scalar.wait()
    pad = jnp.zeros((64, 128), BF)
    for u in range(4):
        own_blocks[u, 0:64] = packs[u, 512:576]
        own_blocks[u, 64:128] = pad
        own_blocks[u, 128:256] = jnp.concatenate([packs[u, 576:640], pad], axis=0).T

    def attend(t, units):
        n = len(CHUNKS[t])
        for u in units:
            odd_prompt = lax.rem(owner_s[2 * u + c, 0], 2)
            keys = [kvs[t][odd_prompt, i, 0:128] for i in range(n)]
            if t == 0:
                keys.append(own_blocks[u, 0:128])
            keys = jnp.concatenate(keys, axis=0)
            scores = lax.dot_general(
                keys, packs[u, 0:512], (((1,), (1,)), ((), ())), preferred_element_type=F32
            )
            if t == 0:
                row = lax.broadcasted_iota(jnp.int32, (128, 512), 0)
                position = lax.broadcasted_iota(jnp.int32, (128, 512), 1) & 63
                mine = jnp.where(row <= position, scores[n * 128 :], -1e30)
                scores = jnp.concatenate([scores[: n * 128], mine], axis=0)
            high = jnp.max(scores, axis=0, keepdims=True) * LOG2E_SCALE
            if t > 0:
                before = m_s[u, t - 1 : t]
                high = jnp.maximum(before, high)
            weights = jnp.exp2(scores * LOG2E_SCALE - high)
            total = jnp.sum(weights, axis=0, keepdims=True)
            if t > 0:
                total = l_s[u, 0:1] * jnp.exp2(before - high) + total
            m_s[u, t : t + 1] = high
            l_s[u, 0:1] = total
            probs[u, STARTS[t] : STARTS[t + 1]] = weights

    def weigh(u):
        odd_prompt = lax.rem(owner_s[2 * u + c, 0], 2)
        last, inverse = m_s[u, 3:4], 1.0 / l_s[u, 0:1]
        out = jnp.zeros((128, 512), F32)
        for t in range(4):
            values = [kvs[t][odd_prompt, i, 128:256] for i in range(len(CHUNKS[t]))]
            if t == 0:
                values.append(own_blocks[u, 128:256])
            share = jnp.exp2(m_s[u, t : t + 1] - last) * inverse
            weights = (probs[u, STARTS[t] : STARTS[t + 1]] * share).astype(BF)
            out = out + jnp.dot(jnp.concatenate(values, axis=1), weights, preferred_element_type=F32)
        att_send[u] = out.T.astype(BF)

    def chunk_ready(t):
        for slot in CHUNKS[t]:
            sib_ref = kvs[t].at[1 - c, PLACE[slot][1]]
            remote(sib_ref, sib_ref, sib_ss.at[slot], sib_rs.at[slot], sibling).wait_recv()

    kv_hop(4)
    chunk_ready(0)
    attend(0, (0, 1))
    kv_hop(5)
    attend(0, (2, 3))
    early_w.wait()
    for way in (0, 1):
        launch(w_copy(way, 1))
    launch(w_sib(0, 0, c))
    kv_hop(6)
    chunk_ready(1)
    attend(1, (0, 1))
    kv_hop(7)
    attend(1, (2, 3))
    w_hop(1)
    kv_hop(8)
    chunk_ready(2)
    attend(2, (0, 1, 2, 3))
    w_hop(2)
    chunk_ready(3)
    attend(3, (0, 1, 2, 3))

    def att_copy(d, half):
        heads = pl.ds(pl.multiple_of(lax.rem(x + d, 4) * 2 * RT, 2 * RT), 2 * RT)
        return remote(
            att_send.at[pl.ds(2 * half, 2), heads, :], att_recv.at[x, pl.ds(2 * half, 2)],
            a_ss.at[d - 1, half], a_rs.at[d - 1, half], along_x(d),
        )

    for half in (0, 1):
        weigh(2 * half)
        weigh(2 * half + 1)
        for d in (2, 1, 3):
            launch(att_copy(d, half))
        w_hop(3 + half)
    att_recv[x] = att_send[:, pl.ds(pl.multiple_of(x * 2 * RT, 2 * RT), 2 * RT), :]
    for half in (0, 1):
        for d in (1, 3, 2):
            ref = att_recv.at[lax.rem(x + 4 - d, 4), pl.ds(2 * half, 2)]
            remote(ref, ref, a_ss.at[d - 1, half], a_rs.at[d - 1, half], along_x(d)).wait_recv()
    for u in range(4):
        heads = att_recv[lax.div(owner_s[2 * u + c, 0], 2), u]
        for h in (0, 1):
            att[h, u * RT : (u + 1) * RT] = heads[h * RT : (h + 1) * RT]

    def first(k, kind):
        step = 1 if kind < 3 else 3
        return remote(
            send1.at[k, kind], recv1.at[k, kind], f_ss.at[k, kind], f_rs.at[k, kind],
            along_x(step) if X_FIRST[k] else along_y(step),
        )

    def second(k, d):
        me, device = (v, along_y(d)) if X_FIRST[k] else (x, along_x(d))
        return remote(
            send2.at[k, lax.rem(me + d, 4)], recv2.at[k, d - 1], g_ss.at[k, d - 1], g_rs.at[k, d - 1], device
        )

    def normed_copy(k, d, from_me=True):
        ref = hidden_c.at[k, v if from_me else lax.rem(v + 4 - d, 4)]
        return remote(ref, ref, n_ss.at[k, d - 1], n_rs.at[k, d - 1], along_y(d))

    def chunk(k):
        return lax.rem(lax.div(s, 2) + ORDER[k], 8)

    def columns_of(k):
        return pl.ds(pl.multiple_of(chunk(k) * CW, CW), CW)

    def project(h, k):
        columns = jnp.concatenate([w_slots[h, 2 * chunk(k)], w_slots[h, 2 * chunk(k) + 1]], axis=0)
        return lax.dot_general(att[h], columns, (((1,), (1,)), ((), ())), preferred_element_type=F32)

    def step1(k):
        total = project(0, k) + project(1, k)
        if X_FIRST[k]:
            pieces = [total[i * 64 : (i + 1) * 64] for i in range(4)]
        else:
            pieces = [
                jnp.concatenate([total[j * 64 + i * 16 : j * 64 + i * 16 + 16] for j in range(4)], axis=0)
                for i in range(4)
            ]
        for i in range(4):
            tmp1[i] = pieces[i]
        me = x if X_FIRST[k] else v
        after, opposite, before = lax.rem(me + 1, 4), lax.rem(me + 2, 4), lax.rem(me + 3, 4)
        for kind, piece, rows in (
            (0, opposite, slice(0, 32)), (3, opposite, slice(32, 64)), (1, after, slice(32, 64)), (4, before, slice(0, 32))
        ):
            send1[k, kind] = encode(tmp1[piece, rows])
            launch(first(k, kind))
        kept[k, 0:32] = tmp1[after, 0:32]
        kept[k, 32:64] = tmp1[before, 32:64]
        own1[k] = tmp1[me]

    def relay(k):
        for kind, rows in ((0, slice(0, 32)), (3, slice(32, 64))):
            first(k, kind).wait_recv()
            send1[k, kind + 2] = encode(kept[k, rows] + decode(recv1[k, kind]))
            launch(first(k, kind + 2))

    def step2(k):
        for kind in (1, 4, 2, 5):
            first(k, kind).wait_recv()
        total = own1[k] + jnp.concatenate(
            [decode(recv1[k, 4]) + decode(recv1[k, 2]), decode(recv1[k, 1]) + decode(recv1[k, 5])], axis=0
        )
        coded = encode(total)
        for i in range(4):
            tmp2[i] = total[i * 16 : (i + 1) * 16]
            send2[k, i] = coded[i * 16 : (i + 1) * 16]
        for d in (1, 3, 2):
            launch(second(k, d))
        own2[k] = tmp2[v if X_FIRST[k] else x]

    def step3(k, square):
        total = own2[k]
        for d in (1, 3, 2):
            second(k, d).wait_recv()
        for d in (1, 3, 2):
            total = total + decode(recv2[k, d - 1])
        hidden = resid_v[:, columns_of(k)].astype(F32) + total
        for i in range(CW // 128):
            part = hidden[:, i * 128 : (i + 1) * 128]
            square = square + part * part
        hidden_c[k, v] = encode(hidden)
        for d in (1, 3, 2):
            launch(normed_copy(k, d))
        return square

    def step4(k):
        for d in (1, 3, 2):
            normed_copy(k, d, False).wait_recv()
        hidden_v[k] = decode(jnp.concatenate([hidden_c[k, i] for i in range(4)], axis=0))

    def step5(k, scale, logits):
        tiles = [
            (hidden_v[k, :, i * 128 : (i + 1) * 128] * scale * gain_v[chunk(k), i : i + 1]).astype(BF)
            for i in range(CW // 128)
        ]
        return logits + lax.dot_general(
            head_v[:, columns_of(k)], jnp.concatenate(tiles, axis=1), (((1,), (1,)), ((), ())),
            preferred_element_type=F32,
        )

    square = jnp.zeros((16, 128), F32)
    for hop in (0, 1):
        w_ready(hop)
    step1(0)
    for hop in (2, 3):
        w_ready(hop)
    step1(1)
    w_hop(5)
    step1(2)
    relay(0)
    for hop in (4, 5):
        w_ready(hop)
    step1(3)
    w_hop(6)
    relay(1)
    step1(4)
    relay(2)
    w_hop(7)
    for copy in late:
        copy.wait()
    for i in range(NCH):
        gain_v[i, 0:5] = gain_in[i * 5 : i * 5 + 5].astype(F32)
    step2(0)
    relay(3)
    step2(1)
    for hop in (6, 7):
        w_ready(hop)
    step1(5)
    step2(2)
    w_hop(8)
    square = step3(0, square)
    relay(4)
    step2(3)
    step1(6)
    square = step3(1, square)
    square = step3(2, square)
    relay(5)
    step2(4)
    w_ready(8)
    step1(7)
    square = step3(3, square)
    step4(0)
    step4(1)
    step4(2)
    for k in range(5, NCH):
        if k + 1 < NCH:
            relay(k + 1)
        step2(k)
        square = step3(k - 1, square)
        step4(k - 2)
    square = step3(NCH - 1, square)
    squares[v] = square
    for d in (1, 3, 2):
        launch(remote(squares.at[v], squares.at[v], t_ss.at[d - 1], t_rs.at[d - 1], along_y(d)))
    step4(6)
    step4(7)
    for d in (1, 3, 2):
        ref = squares.at[lax.rem(v + 4 - d, 4)]
        remote(ref, ref, t_ss.at[d - 1], t_rs.at[d - 1], along_y(d)).wait_recv()
    rows = jnp.concatenate([squares[i] for i in range(4)], axis=0)
    mean = jnp.broadcast_to(jnp.sum(rows, axis=1, keepdims=True) * (1.0 / D), (RT, 128))
    scale = lax.rsqrt(mean + 1e-06)
    logits = jnp.zeros((256, RT), F32)
    for k in range(NCH):
        logits = step5(k, scale, logits)

    high = jnp.max(logits, axis=0, keepdims=True)
    total = jnp.sum(jnp.exp(logits - high), axis=0, keepdims=True)
    entry = lax.broadcasted_iota(jnp.int32, (256, RT), 0) + v * 256
    picked = jnp.sum(jnp.where(entry == tok_v[0], logits, 0.0), axis=0, keepdims=True)
    stats[0, 0:1, 0:RT] = high
    stats[0, 1:2, 0:RT] = total
    stats[0, 2:3, 0:RT] = picked
    for d in (1, 3, 2):
        launch(remote(stats.at[0], stats.at[d], e_ss.at[d - 1], e_rs.at[d - 1], along_y(d)))
    for d in (1, 3, 2):
        remote(stats.at[0], stats.at[d], e_ss.at[d - 1], e_rs.at[d - 1], along_y(d)).wait_recv()
    highs = [high] + [stats[d, 0:1, 0:RT] for d in (1, 2, 3)]
    totals = [total] + [stats[d, 1:2, 0:RT] for d in (1, 2, 3)]
    target = picked + stats[1, 2:3, 0:RT] + stats[2, 2:3, 0:RT] + stats[3, 2:3, 0:RT]
    highest = functools.reduce(jnp.maximum, highs)
    exp_total = functools.reduce(jnp.add, [a * jnp.exp(b - highest) for a, b in zip(totals, highs)])
    logprob = target - (highest + jnp.log(exp_total))
    delta = jnp.clip(logprob - pol_v[0], -20.0, 20.0)
    divergence = jnp.clip(jnp.exp(delta) - delta - 1.0, -10.0, 10.0)
    out_ref[0, 0:1] = logprob
    out_ref[0, 1:2] = divergence
    for copy in sends:
        copy.wait_send()


def local(prompt_kv, owner, queries, resp_kv, lengths, out_proj, resid, gain, head_w, token_ids, pol_logprobs):
    vmem, hbm = pl.BlockSpec(memory_space=pltpu.VMEM), pl.BlockSpec(memory_space=pltpu.HBM)
    dma = pltpu.SemaphoreType.DMA
    wide = CW + 128
    scratch = [
        *[pltpu.VMEM((2, len(slots), 256, 128), BF) for slots in CHUNKS],
        pltpu.VMEM((4, 640, 128), BF),
        pltpu.VMEM((4, 256, 128), BF),
        pltpu.SMEM((1, 16), jnp.int32),
        pltpu.VMEM((8, 128), jnp.int32),
        pltpu.SMEM((8, 128), jnp.int32),
        pltpu.VMEM((4, 8, 512), F32),
        pltpu.VMEM((4, 8, 512), F32),
        pltpu.VMEM((4, STARTS[4], 512), F32),
        pltpu.VMEM((4, 512, 128), BF),
        pltpu.VMEM((4, 4, 2 * RT, 128), BF),
        pltpu.VMEM((2, 256, 128), BF),
        pltpu.VMEM((128, 128), BF),
        pltpu.VMEM((2, 16, 320, 128), BF),
        pltpu.VMEM((4, 64, CW), F32),
        pltpu.VMEM((NCH, 64, CW), F32),
        pltpu.VMEM((NCH, 64, CW), F32),
        pltpu.VMEM((NCH, 6, 32, wide), jnp.int16),
        pltpu.VMEM((NCH, 6, 32, wide), jnp.int16),
        pltpu.VMEM((4, 16, CW), F32),
        pltpu.VMEM((NCH, 16, CW), F32),
        pltpu.VMEM((NCH, 4, 16, wide), jnp.int16),
        pltpu.VMEM((NCH, 3, 16, wide), jnp.int16),
        pltpu.VMEM((16, D), BF),
        pltpu.VMEM((256, D), BF),
        pltpu.VMEM((D // 128, 128), BF),
        pltpu.VMEM((NCH, 8, 128), F32),
        pltpu.VMEM((1, 1, RT), jnp.int32),
        pltpu.VMEM((1, 1, RT), F32),
        pltpu.VMEM((NCH, 4, 16, wide), jnp.int16),
        pltpu.VMEM((NCH, RT, CW), F32),
        pltpu.VMEM((4, 16, 128), F32),
        pltpu.VMEM((4, 8, 128), F32),
        dma((21,)),
    ]
    for shape in ((3,), (3,), (2, 8, 2), (16,), (2, 8), (16,), (3, 2), (NCH, 6), (NCH, 3), (NCH, 3), (3,), (3,)):
        scratch += [dma(shape), dma(shape)]
    scored = pl.pallas_call(
        kernel,
        out_shape=jax.ShapeDtypeStruct((1, 2, RT), F32),
        in_specs=[hbm] * 10,
        out_specs=vmem,
        scratch_shapes=scratch,
        compiler_params=pltpu.CompilerParams(
            collective_id=0, has_side_effects=True, vmem_limit_bytes=60 * 1024 * 1024
        ),
        name="score",
    )(
        prompt_kv, owner, queries, resp_kv, out_proj.T, resid, gain.reshape(D // 128, 128), head_w, token_ids,
        pol_logprobs,
    )
    live = lax.broadcasted_iota(jnp.int32, (1, 1, RT), 2) < lengths[0, 0]
    return jnp.where(live, scored[:, 0:1], 0.0), jnp.where(live, scored[:, 1:2], 0.0)


def solution(mesh):
    in_specs = (
        P("grp", "seq", "voc"),
        P("grp", None),
        P("grp", "seq", None, "voc"),
        P("grp", "seq", None, "voc"),
        P("grp", "seq"),
        P("voc", "seq"),
        P("grp", "seq", None, None),
        P(),
        P("voc", None),
        P("grp", "seq", None),
        P("grp", "seq", None),
    )
    out_specs = (P("grp", "seq", None), P("grp", "seq", None))
    return jax.shard_map(local, mesh=mesh, in_specs=in_specs, out_specs=out_specs, check_vma=False)
```

```python
import functools
import math

import jax
import jax.numpy as jnp
from jax import lax
from jax.experimental import pallas as pl
from jax.experimental.pallas import tpu as pltpu
from jax.sharding import PartitionSpec as P

MESH = pl.DeviceIdType.MESH
HD = 128
RT = 64
D = 5120
CW = 640
NCH = D // CW
BF = jnp.bfloat16
F32 = jnp.float32
LOG2E_SCALE = math.log2(math.e) / math.sqrt(HD)
CHUNKS = ((0, 1, 2, 3, 4), (5, 6, 7, 8), (9, 10, 11, 12), (13, 14, 15))
STARTS = (0, 768, 1280, 1792, 2176)
X_FIRST = (False, True, False, True, True, False, True, True)
ORDER = (0, 1, 7, 2, 6, 3, 5, 4)
PLACE = {slot: (t, i) for t, slots in enumerate(CHUNKS) for i, slot in enumerate(slots)}


def slot_of(way, hop):
    return 0 if hop == 0 else 15 if hop == 8 else 2 * hop - 1 + way


def lanes_max(rows):
    high = jnp.abs(rows[:, 0:128])
    for i in range(128, rows.shape[1], 128):
        high = jnp.maximum(high, jnp.abs(rows[:, i : i + 128]))
    return jnp.broadcast_to(jnp.max(high, axis=1, keepdims=True), high.shape)


def scaled_rows(rows):
    exponent = jnp.ceil(jnp.log2(jnp.maximum(lanes_max(rows), 1e-30)) + 0.01)
    scale = jnp.exp2(-exponent) * 32000.0
    return jnp.round(rows * jnp.concatenate([scale] * (CW // 128), axis=1)), exponent


def restored(values, exponent):
    scale = jnp.exp2(exponent) * (1.0 / 32000.0)
    return values.astype(F32) * jnp.concatenate([scale] * (CW // 128), axis=1)


def encode(rows):
    return jnp.concatenate(scaled_rows(rows), axis=1).astype(jnp.int16)


def decode(coded):
    return restored(coded[:, :CW], coded[:, CW:].astype(F32))


def encode_pair(rows):
    values, exponent = scaled_rows(rows)
    left = lax.broadcasted_iota(jnp.int32, (16, 128), 1) < 64
    both = jnp.where(left, exponent[0:16], exponent[16:32])
    return jnp.concatenate([values[0:16], values[16:32], both], axis=1).astype(jnp.int16)


def decode_pair(coded):
    both = coded[:, 2 * CW :].astype(F32)
    turned = jnp.concatenate([both[:, 64:], both[:, :64]], axis=1)
    left = lax.broadcasted_iota(jnp.int32, (16, 128), 1) < 64
    return jnp.concatenate(
        [
            restored(coded[:, :CW], jnp.where(left, both, turned)),
            restored(coded[:, CW : 2 * CW], jnp.where(left, turned, both)),
        ],
        axis=0,
    )


def kernel(
    kv_ref, owner_ref, q_ref, own_ref, proj_ref, resid_ref, gain_ref, head_ref, tok_ref, pol_ref,
    out_ref,
    kv0, kv1, kv2, kv3, packs, own_blocks, owner_in, owner_v, owner_s, m_s, l_s, probs, att_send, att_recv, att,
    v_in, w_slots, tmp1, own1, kept, send1, recv1, tmp2, own2, send2, recv2,
    resid_v, head_v, gain_in, gain_v, tok_v, pol_v, hidden_c, hidden_v, squares, stats, load_sem,
    q_ss, q_rs, o_ss, o_rs, kv_ss, kv_rs, sib_ss, sib_rs, w_ss, w_rs, wb_ss, wb_rs, a_ss, a_rs,
    f_ss, f_rs, g_ss, g_rs, n_ss, n_rs, t_ss, t_rs, e_ss, e_rs,
):
    g, s, v = lax.axis_index("grp"), lax.axis_index("seq"), lax.axis_index("voc")
    x, c = lax.div(g, 2), lax.rem(g, 2)
    kvs = (kv0, kv1, kv2, kv3)
    sends = []

    def remote(src, dst, ss, rs, device):
        return pltpu.make_async_remote_copy(
            src_ref=src, dst_ref=dst, send_sem=ss, recv_sem=rs, device_id=device, device_id_type=MESH
        )

    def launch(copy):
        copy.start()
        sends.append(copy)

    def along_x(d):
        return {"grp": lax.rem(g + 2 * d, 8)}

    def along_y(d):
        return {"voc": lax.rem(v + d, 4)}

    def along_z(way):
        return {"seq": lax.rem(s + (1 if way == 0 else 15), 16)}

    sibling = {"grp": 2 * x + 1 - c}

    barrier = pltpu.get_barrier_semaphore()
    for device in [along_x(d) for d in range(1, 4)] + [along_y(d) for d in range(1, 4)] + [along_z(0), along_z(1), sibling]:
        pl.semaphore_signal(barrier, inc=1, device_id=device, device_id_type=MESH)

    def load(index, src, dst):
        copy = pltpu.make_async_copy(src, dst, load_sem.at[index])
        copy.start()
        return copy

    early = [
        load(1, kv_ref.at[0, :, pl.ds(HD, HD)], v_in),
        load(2, kv_ref.at[0, :, pl.ds(0, HD)], kv0.at[c, 0, pl.ds(0, HD)]),
    ]
    early_owner = load(0, owner_ref, owner_in)
    early_q = [load(3 + j, q_ref.at[0, 0, :, pl.ds(j * HD, HD)], packs.at[x, pl.ds(j * RT, RT)]) for j in range(8)]
    early_q += [load(11 + j, own_ref.at[0, 0, :, pl.ds(j * HD, HD)], packs.at[x, pl.ds(512 + j * RT, RT)]) for j in range(2)]
    early_w = load(13, proj_ref.at[:, pl.ds(pl.multiple_of(g * HD, HD), HD)], w_slots.at[c, s])
    late = [
        load(14, resid_ref.at[0, 0, pl.ds(pl.multiple_of(v * 16, 16), 16), :], resid_v),
        load(15, head_ref, head_v),
        load(16, gain_ref, gain_in),
        load(17, tok_ref, tok_v),
        load(18, pol_ref, pol_v),
    ]
    for copy in early:
        copy.wait()
    kv0[c, 0, 128:256] = v_in[...].T

    pl.semaphore_wait(barrier, 9)

    def kv_piece(slot, sub):
        t, i = PLACE[slot]
        return kvs[t].at[c, i, pl.ds(sub * 128, 128)]

    def kv_copy(way, hop, sub):
        return remote(
            kv_piece(slot_of(way, hop - 1), sub), kv_piece(slot_of(way, hop), sub),
            kv_ss.at[way, hop - 1, sub], kv_rs.at[way, hop - 1, sub], along_z(way),
        )

    def kv_subs(way, hop):
        return (0, 1) if hop < 8 else (way,)

    def sib_copy(slot):
        t, i = PLACE[slot]
        return remote(kvs[t].at[c, i], kvs[t].at[c, i], sib_ss.at[slot], sib_rs.at[slot], sibling)

    def kv_hop(hop):
        for sub in (0, 1):
            for way in (0, 1):
                if sub in kv_subs(way, hop):
                    kv_copy(way, hop, sub).wait_recv()
                    if hop < 8 and sub in kv_subs(way, hop + 1):
                        launch(kv_copy(way, hop + 1, sub))
        for slot in sorted({slot_of(0, hop), slot_of(1, hop)}):
            launch(sib_copy(slot))

    def w_piece(way, hop, which):
        index = lax.rem(s + (16 - hop if way == 0 else hop), 16)
        if which == 8:
            return w_slots.at[c, index, pl.ds(way * 160, 160)]
        return w_slots.at[c, index]

    def w_copy(way, hop):
        return remote(
            w_piece(way, hop - 1, hop), w_piece(way, hop - 1, hop), w_ss.at[way, hop - 1], w_rs.at[way, hop - 1],
            along_z(way),
        )

    def w_arrived(way, hop):
        ref = w_piece(way, hop, hop)
        return remote(ref, ref, w_ss.at[way, hop - 1], w_rs.at[way, hop - 1], along_z(way))

    def w_hop(hop):
        for way in (0, 1):
            w_arrived(way, hop).wait_recv()
            if hop < 8:
                launch(w_copy(way, hop + 1))
        for way in (0, 1) if hop < 8 else (0,):
            launch(w_sib(way, hop, c))

    def w_sib(way, hop, head):
        ref = w_slots.at[head, lax.rem(s + (16 - hop if way == 0 else hop), 16)]
        slot = slot_of(way, hop)
        return remote(ref, ref, wb_ss.at[slot], wb_rs.at[slot], sibling)

    def w_ready(hop):
        for way in (0, 1) if 0 < hop < 8 else (0,):
            w_sib(way, hop, 1 - c).wait_recv()

    for sub in (0, 1):
        for way in (0, 1):
            launch(kv_copy(way, 1, sub))
    launch(sib_copy(0))
    for copy in early_q:
        copy.wait()
    for d in (1, 3, 2):
        launch(remote(packs.at[x], packs.at[x], q_ss.at[d - 1], q_rs.at[d - 1], along_x(d)))
    early_owner.wait()
    owner_v[pl.ds(g, 1), :] = jnp.full((1, 128), owner_in[0, s], jnp.int32)
    for d in (1, 3, 2):
        row = owner_v.at[pl.ds(g, 1)]
        launch(remote(row, row, o_ss.at[d - 1], o_rs.at[d - 1], along_x(d)))

    kv_hop(1)
    kv_hop(2)
    kv_hop(3)

    for d in (1, 3, 2):
        row = owner_v.at[pl.ds(lax.rem(g + 8 - 2 * d, 8), 1)]
        remote(row, row, o_ss.at[d - 1], o_rs.at[d - 1], along_x(d)).wait_recv()
    to_scalar = pltpu.make_async_copy(owner_v, owner_s, load_sem.at[20])
    to_scalar.start()
    for d in (1, 3, 2):
        ref = packs.at[lax.rem(x + 4 - d, 4)]
        remote(ref, ref, q_ss.at[d - 1], q_rs.at[d - 1], along_x(d)).wait_recv()
    to_scalar.wait()
    pad = jnp.zeros((64, 128), BF)
    for u in range(4):
        own_blocks[u, 0:64] = packs[u, 512:576]
        own_blocks[u, 64:128] = pad
        own_blocks[u, 128:256] = jnp.concatenate([packs[u, 576:640], pad], axis=0).T

    def attend(t, units):
        n = len(CHUNKS[t])
        for u in units:
            odd_prompt = lax.rem(owner_s[2 * u + c, 0], 2)
            keys = [kvs[t][odd_prompt, i, 0:128] for i in range(n)]
            if t == 0:
                keys.append(own_blocks[u, 0:128])
            keys = jnp.concatenate(keys, axis=0)
            scores = lax.dot_general(
                keys, packs[u, 0:512], (((1,), (1,)), ((), ())), preferred_element_type=F32
            )
            if t == 0:
                row = lax.broadcasted_iota(jnp.int32, (128, 512), 0)
                position = lax.broadcasted_iota(jnp.int32, (128, 512), 1) & 63
                mine = jnp.where(row <= position, scores[n * 128 :], -1e30)
                scores = jnp.concatenate([scores[: n * 128], mine], axis=0)
            high = jnp.max(scores, axis=0, keepdims=True) * LOG2E_SCALE
            if t > 0:
                before = m_s[u, t - 1 : t]
                high = jnp.maximum(before, high)
            weights = jnp.exp2(scores * LOG2E_SCALE - high)
            total = jnp.sum(weights, axis=0, keepdims=True)
            if t > 0:
                total = l_s[u, 0:1] * jnp.exp2(before - high) + total
            m_s[u, t : t + 1] = high
            l_s[u, 0:1] = total
            probs[u, STARTS[t] : STARTS[t + 1]] = weights

    def weigh(u):
        odd_prompt = lax.rem(owner_s[2 * u + c, 0], 2)
        last, inverse = m_s[u, 3:4], 1.0 / l_s[u, 0:1]
        out = jnp.zeros((128, 512), F32)
        for t in range(4):
            values = [kvs[t][odd_prompt, i, 128:256] for i in range(len(CHUNKS[t]))]
            if t == 0:
                values.append(own_blocks[u, 128:256])
            share = jnp.exp2(m_s[u, t : t + 1] - last) * inverse
            weights = (probs[u, STARTS[t] : STARTS[t + 1]] * share).astype(BF)
            out = out + jnp.dot(jnp.concatenate(values, axis=1), weights, preferred_element_type=F32)
        att_send[u] = out.T.astype(BF)

    def chunk_ready(t):
        for slot in CHUNKS[t]:
            sib_ref = kvs[t].at[1 - c, PLACE[slot][1]]
            remote(sib_ref, sib_ref, sib_ss.at[slot], sib_rs.at[slot], sibling).wait_recv()

    kv_hop(4)
    chunk_ready(0)
    attend(0, (0, 1))
    kv_hop(5)
    attend(0, (2, 3))
    early_w.wait()
    for way in (0, 1):
        launch(w_copy(way, 1))
    launch(w_sib(0, 0, c))
    kv_hop(6)
    chunk_ready(1)
    attend(1, (0, 1))
    kv_hop(7)
    attend(1, (2, 3))
    w_hop(1)
    kv_hop(8)
    chunk_ready(2)
    attend(2, (0, 1, 2, 3))
    w_hop(2)
    chunk_ready(3)
    attend(3, (0, 1, 2, 3))

    def att_copy(d, half):
        heads = pl.ds(pl.multiple_of(lax.rem(x + d, 4) * 2 * RT, 2 * RT), 2 * RT)
        return remote(
            att_send.at[pl.ds(2 * half, 2), heads, :], att_recv.at[x, pl.ds(2 * half, 2)],
            a_ss.at[d - 1, half], a_rs.at[d - 1, half], along_x(d),
        )

    for half in (0, 1):
        weigh(2 * half)
        weigh(2 * half + 1)
        for d in (2, 1, 3):
            launch(att_copy(d, half))
        w_hop(3 + half)
    att_recv[x] = att_send[:, pl.ds(pl.multiple_of(x * 2 * RT, 2 * RT), 2 * RT), :]
    for half in (0, 1):
        for d in (1, 3, 2):
            ref = att_recv.at[lax.rem(x + 4 - d, 4), pl.ds(2 * half, 2)]
            remote(ref, ref, a_ss.at[d - 1, half], a_rs.at[d - 1, half], along_x(d)).wait_recv()
    for u in range(4):
        heads = att_recv[lax.div(owner_s[2 * u + c, 0], 2), u]
        for h in (0, 1):
            att[h, u * RT : (u + 1) * RT] = heads[h * RT : (h + 1) * RT]

    def first(k, kind):
        step = 1 if kind < 3 else 3
        return remote(
            send1.at[k, kind], recv1.at[k, kind], f_ss.at[k, kind], f_rs.at[k, kind],
            along_x(step) if X_FIRST[k] else along_y(step),
        )

    def second(k, d):
        me, device = (v, along_y(d)) if X_FIRST[k] else (x, along_x(d))
        return remote(
            send2.at[k, lax.rem(me + d, 4)], recv2.at[k, d - 1], g_ss.at[k, d - 1], g_rs.at[k, d - 1], device
        )

    def normed_copy(k, d, from_me=True):
        ref = hidden_c.at[k, v if from_me else lax.rem(v + 4 - d, 4)]
        return remote(ref, ref, n_ss.at[k, d - 1], n_rs.at[k, d - 1], along_y(d))

    def chunk(k):
        return lax.rem(lax.div(s, 2) + ORDER[k], 8)

    def columns_of(k):
        return pl.ds(pl.multiple_of(chunk(k) * CW, CW), CW)

    def project(h, k):
        columns = jnp.concatenate([w_slots[h, 2 * chunk(k)], w_slots[h, 2 * chunk(k) + 1]], axis=0)
        return lax.dot_general(att[h], columns, (((1,), (1,)), ((), ())), preferred_element_type=F32)

    def step1(k):
        total = project(0, k) + project(1, k)
        if X_FIRST[k]:
            pieces = [total[i * 64 : (i + 1) * 64] for i in range(4)]
        else:
            pieces = [
                jnp.concatenate([total[j * 64 + i * 16 : j * 64 + i * 16 + 16] for j in range(4)], axis=0)
                for i in range(4)
            ]
        for i in range(4):
            tmp1[i] = pieces[i]
        me = x if X_FIRST[k] else v
        after, opposite, before = lax.rem(me + 1, 4), lax.rem(me + 2, 4), lax.rem(me + 3, 4)
        for kind, piece, rows in (
            (0, opposite, slice(0, 32)), (3, opposite, slice(32, 64)), (1, after, slice(32, 64)), (4, before, slice(0, 32))
        ):
            send1[k, kind] = encode_pair(tmp1[piece, rows])
            launch(first(k, kind))
        kept[k, 0:32] = tmp1[after, 0:32]
        kept[k, 32:64] = tmp1[before, 32:64]
        own1[k] = tmp1[me]

    def relay(k):
        for kind, rows in ((0, slice(0, 32)), (3, slice(32, 64))):
            first(k, kind).wait_recv()
            send1[k, kind + 2] = encode_pair(kept[k, rows] + decode_pair(recv1[k, kind]))
            launch(first(k, kind + 2))

    def step2(k):
        for kind in (1, 4, 2, 5):
            first(k, kind).wait_recv()
        total = own1[k] + jnp.concatenate(
            [decode_pair(recv1[k, 4]) + decode_pair(recv1[k, 2]), decode_pair(recv1[k, 1]) + decode_pair(recv1[k, 5])], axis=0
        )
        coded = encode(total)
        for i in range(4):
            tmp2[i] = total[i * 16 : (i + 1) * 16]
            send2[k, i] = coded[i * 16 : (i + 1) * 16]
        for d in (1, 3, 2):
            launch(second(k, d))
        own2[k] = tmp2[v if X_FIRST[k] else x]

    def step3(k, square):
        total = own2[k]
        for d in (1, 3, 2):
            second(k, d).wait_recv()
        for d in (1, 3, 2):
            total = total + decode(recv2[k, d - 1])
        hidden = resid_v[:, columns_of(k)].astype(F32) + total
        for i in range(CW // 128):
            part = hidden[:, i * 128 : (i + 1) * 128]
            square = square + part * part
        hidden_c[k, v] = encode(hidden)
        for d in (1, 3, 2):
            launch(normed_copy(k, d))
        return square

    def step4(k):
        for d in (1, 3, 2):
            normed_copy(k, d, False).wait_recv()
        hidden_v[k] = decode(jnp.concatenate([hidden_c[k, i] for i in range(4)], axis=0))

    def step5(k, scale, logits):
        tiles = [
            (hidden_v[k, :, i * 128 : (i + 1) * 128] * scale * gain_v[chunk(k), i : i + 1]).astype(BF)
            for i in range(CW // 128)
        ]
        return logits + lax.dot_general(
            head_v[:, columns_of(k)], jnp.concatenate(tiles, axis=1), (((1,), (1,)), ((), ())),
            preferred_element_type=F32,
        )

    square = jnp.zeros((16, 128), F32)
    for hop in (0, 1):
        w_ready(hop)
    step1(0)
    for hop in (2, 3):
        w_ready(hop)
    step1(1)
    w_hop(5)
    step1(2)
    relay(0)
    for hop in (4, 5):
        w_ready(hop)
    step1(3)
    w_hop(6)
    relay(1)
    step1(4)
    relay(2)
    w_hop(7)
    for copy in late:
        copy.wait()
    for i in range(NCH):
        gain_v[i, 0:5] = gain_in[i * 5 : i * 5 + 5].astype(F32)
    step2(0)
    relay(3)
    step2(1)
    for hop in (6, 7):
        w_ready(hop)
    step1(5)
    step2(2)
    w_hop(8)
    square = step3(0, square)
    relay(4)
    step2(3)
    step1(6)
    square = step3(1, square)
    square = step3(2, square)
    relay(5)
    step2(4)
    w_ready(8)
    step1(7)
    square = step3(3, square)
    step4(0)
    step4(1)
    step4(2)
    for k in range(5, NCH):
        if k + 1 < NCH:
            relay(k + 1)
        step2(k)
        square = step3(k - 1, square)
        step4(k - 2)
    square = step3(NCH - 1, square)
    squares[v] = square
    for d in (1, 3, 2):
        launch(remote(squares.at[v], squares.at[v], t_ss.at[d - 1], t_rs.at[d - 1], along_y(d)))
    step4(6)
    step4(7)
    for d in (1, 3, 2):
        ref = squares.at[lax.rem(v + 4 - d, 4)]
        remote(ref, ref, t_ss.at[d - 1], t_rs.at[d - 1], along_y(d)).wait_recv()
    rows = jnp.concatenate([squares[i] for i in range(4)], axis=0)
    mean = jnp.broadcast_to(jnp.sum(rows, axis=1, keepdims=True) * (1.0 / D), (RT, 128))
    scale = lax.rsqrt(mean + 1e-06)
    logits = jnp.zeros((256, RT), F32)
    for k in range(NCH):
        logits = step5(k, scale, logits)

    high = jnp.max(logits, axis=0, keepdims=True)
    total = jnp.sum(jnp.exp(logits - high), axis=0, keepdims=True)
    entry = lax.broadcasted_iota(jnp.int32, (256, RT), 0) + v * 256
    picked = jnp.sum(jnp.where(entry == tok_v[0], logits, 0.0), axis=0, keepdims=True)
    stats[0, 0:1, 0:RT] = high
    stats[0, 1:2, 0:RT] = total
    stats[0, 2:3, 0:RT] = picked
    for d in (1, 3, 2):
        launch(remote(stats.at[0], stats.at[d], e_ss.at[d - 1], e_rs.at[d - 1], along_y(d)))
    for d in (1, 3, 2):
        remote(stats.at[0], stats.at[d], e_ss.at[d - 1], e_rs.at[d - 1], along_y(d)).wait_recv()
    highs = [high] + [stats[d, 0:1, 0:RT] for d in (1, 2, 3)]
    totals = [total] + [stats[d, 1:2, 0:RT] for d in (1, 2, 3)]
    target = picked + stats[1, 2:3, 0:RT] + stats[2, 2:3, 0:RT] + stats[3, 2:3, 0:RT]
    highest = functools.reduce(jnp.maximum, highs)
    exp_total = functools.reduce(jnp.add, [a * jnp.exp(b - highest) for a, b in zip(totals, highs)])
    logprob = target - (highest + jnp.log(exp_total))
    delta = jnp.clip(logprob - pol_v[0], -20.0, 20.0)
    divergence = jnp.clip(jnp.exp(delta) - delta - 1.0, -10.0, 10.0)
    out_ref[0, 0:1] = logprob
    out_ref[0, 1:2] = divergence
    for copy in sends:
        copy.wait_send()


def local(prompt_kv, owner, queries, resp_kv, lengths, out_proj, resid, gain, head_w, token_ids, pol_logprobs):
    vmem, hbm = pl.BlockSpec(memory_space=pltpu.VMEM), pl.BlockSpec(memory_space=pltpu.HBM)
    dma = pltpu.SemaphoreType.DMA
    wide = CW + 128
    scratch = [
        *[pltpu.VMEM((2, len(slots), 256, 128), BF) for slots in CHUNKS],
        pltpu.VMEM((4, 640, 128), BF),
        pltpu.VMEM((4, 256, 128), BF),
        pltpu.SMEM((1, 16), jnp.int32),
        pltpu.VMEM((8, 128), jnp.int32),
        pltpu.SMEM((8, 128), jnp.int32),
        pltpu.VMEM((4, 8, 512), F32),
        pltpu.VMEM((4, 8, 512), F32),
        pltpu.VMEM((4, STARTS[4], 512), F32),
        pltpu.VMEM((4, 512, 128), BF),
        pltpu.VMEM((4, 4, 2 * RT, 128), BF),
        pltpu.VMEM((2, 256, 128), BF),
        pltpu.VMEM((128, 128), BF),
        pltpu.VMEM((2, 16, 320, 128), BF),
        pltpu.VMEM((4, 64, CW), F32),
        pltpu.VMEM((NCH, 64, CW), F32),
        pltpu.VMEM((NCH, 64, CW), F32),
        pltpu.VMEM((NCH, 6, 16, 2 * CW + 128), jnp.int16),
        pltpu.VMEM((NCH, 6, 16, 2 * CW + 128), jnp.int16),
        pltpu.VMEM((4, 16, CW), F32),
        pltpu.VMEM((NCH, 16, CW), F32),
        pltpu.VMEM((NCH, 4, 16, wide), jnp.int16),
        pltpu.VMEM((NCH, 3, 16, wide), jnp.int16),
        pltpu.VMEM((16, D), BF),
        pltpu.VMEM((256, D), BF),
        pltpu.VMEM((D // 128, 128), BF),
        pltpu.VMEM((NCH, 8, 128), F32),
        pltpu.VMEM((1, 1, RT), jnp.int32),
        pltpu.VMEM((1, 1, RT), F32),
        pltpu.VMEM((NCH, 4, 16, wide), jnp.int16),
        pltpu.VMEM((NCH, RT, CW), F32),
        pltpu.VMEM((4, 16, 128), F32),
        pltpu.VMEM((4, 8, 128), F32),
        dma((21,)),
    ]
    for shape in ((3,), (3,), (2, 8, 2), (16,), (2, 8), (16,), (3, 2), (NCH, 6), (NCH, 3), (NCH, 3), (3,), (3,)):
        scratch += [dma(shape), dma(shape)]
    scored = pl.pallas_call(
        kernel,
        out_shape=jax.ShapeDtypeStruct((1, 2, RT), F32),
        in_specs=[hbm] * 10,
        out_specs=vmem,
        scratch_shapes=scratch,
        compiler_params=pltpu.CompilerParams(
            collective_id=0, has_side_effects=True, vmem_limit_bytes=60 * 1024 * 1024
        ),
        name="score",
    )(
        prompt_kv, owner, queries, resp_kv, out_proj.T, resid, gain.reshape(D // 128, 128), head_w, token_ids,
        pol_logprobs,
    )
    live = lax.broadcasted_iota(jnp.int32, (1, 1, RT), 2) < lengths[0, 0]
    return jnp.where(live, scored[:, 0:1], 0.0), jnp.where(live, scored[:, 1:2], 0.0)


def solution(mesh):
    in_specs = (
        P("grp", "seq", "voc"),
        P("grp", None),
        P("grp", "seq", None, "voc"),
        P("grp", "seq", None, "voc"),
        P("grp", "seq"),
        P("voc", "seq"),
        P("grp", "seq", None, None),
        P(),
        P("voc", None),
        P("grp", "seq", None),
        P("grp", "seq", None),
    )
    out_specs = (P("grp", "seq", None), P("grp", "seq", None))
    return jax.shard_map(local, mesh=mesh, in_specs=in_specs, out_specs=out_specs, check_vma=False)
```
